512 devices in a mesh: dp: 512 (over z, x, y, core).
Axes of the slice: x: 4, y: 8, z: 8, core: 2. Of those that a mesh axis runs over, the one named last changes fastest.
Arguments:
- images: bfloat16 [163840, 1152], P('dp'), may hold values from -6 to 6
- texts: bfloat16 [163840, 640], P('dp'), may hold values from -6 to 6
- head: bfloat16 [1152, 640], replicated, may hold values from -0.1875 to 0.1875
- log_scale: float32 [1], replicated, may hold values from 2 to 2.6
- bias: float32 [1], replicated, may hold values from -4 to -2
Outputs:
- grad_image: bfloat16 [163840, 1152], P('dp')
- grad_text: bfloat16 [163840, 640], P('dp')
- grad_head: bfloat16 [1152, 640], replicated
The draws below stay inside these ranges and needn't reach their ends.
All inputs are finite; a program needn't handle non-finite values.
Results may differ from the reference program's by a relative error of at most 0.0065.
Values may be sent and summed in bfloat16 or wider, within the bound.
No kernel may reach another device: no remote copies, remote signals or barrier semaphores. Data moves between devices by JAX's collectives and lax.ppermute only.
A program may use at most 64 MiB of HBM per device.

```python
import jax
import jax.numpy as jnp
from jax import lax

D = 1152
E = 640
ROWS = 320
STEPS = 4
TOKENS = 163840
N_DP = 512


def block_scale(own_key, extent, shards, low, largest):
    loudness = 1.0
    for dim, blocks in shards:
        draws = jax.random.uniform(jax.random.fold_in(jax.random.fold_in(own_key, 6), dim), (blocks,), jnp.float32, low / len(shards), largest / len(shards))
        loudness = loudness * jnp.repeat(jnp.exp(draws), extent[dim] // blocks).reshape((-1,) + (1,) * (len(extent) - 1 - dim))
    return loudness


def bell_draw(stream_key, shape, scale, most, split=(), kind=jnp.bfloat16):
    entries = scale * jax.random.normal(stream_key, shape, jnp.float32)
    if split:
        entries = entries * block_scale(stream_key, shape, split, -0.22, 0.18)
    return jnp.clip(entries, -most, most).astype(kind)


def setup_inputs(seed: int = 0) -> dict:
    splits = jax.random.split(jax.random.key(seed), 6)
    return {
        "images": bell_draw(splits[0], (TOKENS, D), 1.0, 6.0, ((0, 512),)),
        "texts": bell_draw(splits[1], (TOKENS, E), 1.0, 6.0, ((0, 512),)),
        "head": bell_draw(splits[2], (D, E), D ** -0.5, 0.1875),
        "log_scale": jnp.clip(jax.random.uniform(splits[3], (1,), jnp.float32, 2.0, 2.6), 2.0, 2.6),
        "bias": jnp.clip(jax.random.uniform(splits[4], (1,), jnp.float32, -4.0, -2.0), -4.0, -2.0),
    }


def normalize(values):
    inverse = lax.rsqrt(lax.optimization_barrier(jnp.sum(values * values, axis=-1, keepdims=True)) + 1e-06)
    return (values * inverse, inverse)

def reference(images, texts, head, log_scale, bias):
    temper = jnp.exp(log_scale[0])
    offset = bias[0]
    proj = jnp.dot(images, head, preferred_element_type=jnp.float32)
    img_n, img_inv = normalize(proj)
    img_b = img_n.astype(jnp.bfloat16)
    txt_n, txt_inv = normalize(texts.astype(jnp.float32))
    txt_b = txt_n.astype(jnp.bfloat16)
    width = texts.shape[1]
    img_blocks = img_b.reshape(N_DP, ROWS, width).astype(jnp.float32)
    txt_blocks = txt_b.reshape(N_DP, ROWS, width)
    identity = jnp.eye(ROWS, dtype=jnp.float32)
    d_img = jnp.zeros((N_DP, ROWS, width), jnp.float32)
    d_txt = jnp.zeros((N_DP, ROWS, width), jnp.float32)
    for step in range(STEPS):
        other = jnp.roll(txt_blocks, step, axis=0).astype(jnp.float32)
        dots = jnp.einsum('nre,nqe->nrq', img_blocks, other)
        logit = temper * dots + offset
        target = identity if step == 0 else jnp.zeros_like(identity)
        slope = (temper * (jax.nn.sigmoid(logit) - target)).astype(jnp.bfloat16).astype(jnp.float32)
        d_img = d_img + jnp.einsum('nrq,nqe->nre', slope, other)
        d_other = jnp.einsum('nrq,nre->nqe', slope, img_blocks)
        d_txt = d_txt + jnp.roll(d_other, -step, axis=0)
    d_img = d_img.reshape(-1, width)
    d_txt = d_txt.reshape(-1, width)
    d_proj = ((d_img - img_n * lax.optimization_barrier(jnp.sum(img_n * d_img, axis=-1, keepdims=True))) * img_inv).astype(jnp.bfloat16)
    grad_image = lax.dot_general(d_proj, head, (((1,), (1,)), ((), ())), preferred_element_type=jnp.float32).astype(jnp.bfloat16)
    grad_text = ((d_txt - txt_n * lax.optimization_barrier(jnp.sum(txt_n * d_txt, axis=-1, keepdims=True))) * txt_inv).astype(jnp.bfloat16)
    head_total = lax.dot_general(images, d_proj, (((0,), (0,)), ((), ())), preferred_element_type=jnp.float32)
    grad_head = (head_total * (1.0 / jnp.sqrt(jnp.float32(ROWS)))).astype(jnp.bfloat16)
    return (grad_image, grad_text, grad_head)
```

```python
import jax
import jax.numpy as jnp
from jax import lax
from jax.sharding import Mesh, PartitionSpec as P

ROWS = 320
AXES = ("z", "x", "y", "c")
SIZES = (8, 4, 8, 2)
f32 = jnp.float32
bf16 = jnp.bfloat16


def shifted(value, steps, sources=None):
    count = 512
    sources = range(count) if sources is None else sources
    return lax.ppermute(value, AXES, [(s, (s + steps) % count) for s in sources])


def swapped(value):
    return lax.ppermute(value, "c", [(0, 1), (1, 0)])


def inverse_norm(values):
    return lax.rsqrt(jnp.sum(values * values, axis=-1, keepdims=True) + 1e-06)


def exchange(value, axes):
    return lax.all_to_all(value, axes, 0, 0)


def spread(value, axes, count):
    return exchange(jnp.broadcast_to(value, (count,) + value.shape), axes)


def total(value):
    return jnp.sum(value.astype(f32), axis=0)


def embed(images, head):
    proj = jnp.dot(images, head, preferred_element_type=f32)
    inv = inverse_norm(proj)
    normed = proj * inv
    return normed, inv, normed.astype(bf16)


def dot_t(a, b):
    return lax.dot_general(a, b, (((1,), (1,)), ((), ())), preferred_element_type=f32)


def t_dot(a, b):
    return lax.dot_general(a, b, (((0,), (0,)), ((), ())), preferred_element_type=f32)


def tangent(grad, normed, inv):
    return (grad - normed * jnp.sum(normed * grad, axis=-1, keepdims=True)) * inv


def reduce_head(images_t, d_proj, core):
    rows = images_t.shape[0] // 2
    width = d_proj.shape[1]
    theirs = lax.dynamic_slice_in_dim(images_t, (1 - core) * rows, rows, 0)
    mine = lax.dynamic_slice_in_dim(images_t, core * rows, rows, 0)
    sent = jnp.dot(theirs, d_proj, preferred_element_type=f32).astype(bf16)
    got = swapped(sent)
    part = jnp.dot(mine, d_proj, preferred_element_type=f32)
    part = (part + got.astype(f32)).astype(bf16)
    part = total(exchange(part.reshape(4, rows // 4, width), "x")).astype(bf16)
    tiles = part.reshape(9, 16, 5, 128).transpose(0, 2, 1, 3).reshape(45, 16, 128)
    tiles = jnp.pad(tiles, ((0, 19), (0, 0), (0, 0)))
    factor = 1.0 / jnp.sqrt(jnp.float32(ROWS))
    tile = (total(exchange(tiles, ("z", "y"))) * factor).astype(bf16)
    tiles = spread(tile, ("z", "y"), 64)[:45]
    part = tiles.reshape(9, 5, 16, 128).transpose(0, 2, 1, 3).reshape(rows // 4, width)
    part = spread(part, "x", 4).reshape(rows, width)
    return spread(part, "c", 2).reshape(2 * rows, width)


def shards(images, texts, head, log_scale, bias):
    temper = jnp.exp(log_scale[0])
    offset = bias[0]
    core = lax.axis_index("c")
    texts_prev = shifted(texts, 2)
    images_other = swapped(images)
    images_next = shifted(images, -1, range(0, 512, 2))

    stack = jnp.concatenate([images, images_other, images_next], 0)
    img_n, img_inv, img_b = embed(stack, head)
    images_t = stack.T

    def text(values):
        values = values.astype(f32)
        inv = inverse_norm(values)
        normed = values * inv
        return normed, inv, normed.astype(bf16)

    txt_n, txt_inv, txt_b = text(texts)
    prev_b = text(texts_prev)[2]

    near = 2 * ROWS
    row = lax.broadcasted_iota(jnp.int32, (near, ROWS), 0)
    col = lax.broadcasted_iota(jnp.int32, (near, ROWS), 1)
    target = (row == col).astype(f32)
    keep = jnp.where((row < ROWS) | (core == 0), 1.0, 0.0)
    logit = temper * dot_t(img_b[:near], txt_b) + offset
    slope = (temper * (jax.nn.sigmoid(logit) - target) * keep).astype(bf16)
    logit_prev = temper * dot_t(img_b, prev_b) + offset
    row3 = lax.broadcasted_iota(jnp.int32, (3 * ROWS, ROWS), 0)
    keep3 = jnp.where((row3 < near) | (core == 1), 1.0, 0.0)
    slope_prev = (temper * jax.nn.sigmoid(logit_prev) * keep3).astype(bf16)

    d_near = jnp.dot(slope, txt_b, preferred_element_type=f32)
    d_img = jnp.dot(slope_prev, prev_b, preferred_element_type=f32)
    d_img = d_img + jnp.pad(d_near, ((0, ROWS), (0, 0)))
    d_proj = tangent(d_img, img_n, img_inv).astype(bf16)
    grad_head = reduce_head(images_t, d_proj, core)

    d_txt = t_dot(slope, img_b[:near])
    d_txt_prev = t_dot(slope_prev, img_b)
    d_txt = d_txt + shifted(d_txt_prev, -2)
    grad_text = tangent(d_txt, txt_n, txt_inv).astype(bf16)

    d_own = d_img[:ROWS] + swapped(d_img[ROWS:near]) + shifted(d_img[near:], 1, range(1, 512, 2))
    d_own_proj = tangent(d_own, img_n[:ROWS], img_inv[:ROWS]).astype(bf16)
    grad_image = dot_t(d_own_proj, head).astype(bf16)
    return (grad_image, grad_text, grad_head)


def solution(mesh):
    grid = Mesh(mesh.devices.reshape(SIZES), AXES)
    in_specs = (P(AXES, None), P(AXES, None), P(), P(), P())
    out_specs = (P(AXES, None), P(AXES, None), P())
    return jax.shard_map(shards, mesh=grid, in_specs=in_specs, out_specs=out_specs, check_vma=False)
```

```python
import jax
import jax.numpy as jnp
from jax import lax
from jax.experimental import pallas as pl
from jax.experimental.pallas import tpu as pltpu
from jax.sharding import Mesh, PartitionSpec as P

ROWS = 320
NEAR = 2 * ROWS
ALL = 3 * ROWS
D = 1152
E = 640
HALF = D // 2
AXES = ("zh", "zl", "x", "yh", "yl", "c")
SIZES = (4, 2, 4, 4, 2, 2)
CUBE = ("zl", "x", "yl")
GRID = ("zh", "yh")
SIDE = 16
TILES = 12
COUNT = 512
f32 = jnp.float32
bf16 = jnp.bfloat16


def shifted(value, steps, sources=None):
    sources = range(COUNT) if sources is None else sources
    return lax.ppermute(value, AXES, [(s, (s + steps) % COUNT) for s in sources])


def swapped(value):
    return lax.ppermute(value, "c", [(0, 1), (1, 0)])


def exchange(value, axes):
    return lax.all_to_all(value, axes, 0, 0)


VMEM = pl.BlockSpec(memory_space=pltpu.VMEM)
SMEM = pl.BlockSpec(memory_space=pltpu.SMEM)


def call(body, name, ins, outs, scratch=(), flops=0, after=(), mark=False):
    size = sum(a.size * a.dtype.itemsize for s, a in ins if s is not SMEM)
    if mark:
        outs = (*outs, (SMEM, (1,), jnp.int32))
    n_in, n_after, n_out = len(ins), len(after), len(outs)

    def run(*refs):
        refs = list(refs)
        if mark:
            refs.pop(n_in + n_after + n_out - 1)[0] = 0
        body(*refs[:n_in], *refs[n_in + n_after :])

    got = pl.pallas_call(
        run,
        out_shape=tuple(jax.ShapeDtypeStruct(dims, dtype) for _, dims, dtype in outs),
        in_specs=[s for s, _ in ins] + [SMEM] * n_after,
        out_specs=tuple(s for s, _, _ in outs),
        scratch_shapes=list(scratch),
        compiler_params=pltpu.CompilerParams(vmem_limit_bytes=16_000_000),
        cost_estimate=pl.CostEstimate(flops=flops, bytes_accessed=size, transcendentals=0),
        name=name,
    )(*(a for _, a in ins), *after)
    return got[0] if len(outs) == 1 else got


def dot(a, b):
    return jnp.dot(a, b, preferred_element_type=f32)


def dot_t(a, b):
    return lax.dot_general(a, b, (((1,), (1,)), ((), ())), preferred_element_type=f32)


def t_dot(a, b):
    return lax.dot_general(a, b, (((0,), (0,)), ((), ())), preferred_element_type=f32)


def normalize(values):
    inv = lax.rsqrt(jnp.sum(values * values, axis=-1, keepdims=True) + 1e-06)
    return values * inv, inv


def tangent(grad, normed, inv):
    return (grad - normed * jnp.sum(normed * grad, axis=-1, keepdims=True)) * inv


def slope_of(img_b, txt_b, scal):
    return scal[0] * jax.nn.sigmoid(scal[0] * dot_t(img_b, txt_b) + scal[1])


def near_body(scal, core, images, other, texts, head, img_n, img_inv, img_b, d_near, d_txt, turned, im):
    im[0:ROWS, :] = images[...]
    im[ROWS:NEAR, :] = other[...]
    txt_b = normalize(texts[...].astype(f32))[0].astype(bf16)
    norm, inv = normalize(dot(im[...], head[...]))
    img_n[...] = norm
    img_inv[...] = inv
    img_b[...] = norm.astype(bf16)
    row = lax.broadcasted_iota(jnp.int32, (NEAR, ROWS), 0)
    col = lax.broadcasted_iota(jnp.int32, (NEAR, ROWS), 1)
    target = jnp.where(row == col, scal[0], 0.0)
    slope = slope_of(img_b[...], txt_b, scal) - target
    slope = jnp.where((row < ROWS) | (core[0] == 0), slope, 0.0).astype(bf16)
    d_near[...] = dot(slope, txt_b)
    d_txt[...] = t_dot(slope, img_b[...])
    turned[...] = im[...].T


def next_body(nxt, head, img_n, img_inv, img_b, turned):
    norm, inv = normalize(dot(nxt[...], head[...]))
    img_n[...] = norm
    img_inv[...] = inv
    img_b[...] = norm.astype(bf16)
    turned[...] = nxt[...].T


def prev_body(scal, core, texts, img_n, img_inv, img_b, d_near, turned, next_n, next_inv, next_b, turned_next,
              sent, d_proj, d_own, d_other, d_next, slope):
    text = normalize(texts[...].astype(f32))[0].astype(bf16)
    slope[0:NEAR, :] = slope_of(img_b[...], text, scal).astype(bf16)
    on_second = jnp.where(core[0] == 1, 1.0, 0.0)
    slope[NEAR:ALL, :] = (slope_of(next_b[...], text, scal) * on_second).astype(bf16)
    grad = dot(slope[0:NEAR, :], text) + d_near[...]
    d_own[...] = grad[0:ROWS]
    d_other[...] = grad[ROWS:NEAR]
    d_proj[0:NEAR, :] = tangent(grad, img_n[...], img_inv[...]).astype(bf16)
    grad = dot(slope[NEAR:ALL, :], text)
    d_next[...] = grad.astype(bf16)
    d_proj[NEAR:ALL, :] = tangent(grad, next_n[...], next_inv[...]).astype(bf16)
    rows = pl.ds(pl.multiple_of((1 - core[0]) * HALF, HALF), HALF)
    part = dot(turned[rows, :], d_proj[0:NEAR, :]) + dot(turned_next[rows, :], d_proj[NEAR:ALL, :])
    sent[...] = part.astype(bf16)


def half_body(core, d_proj, turned, turned_next, out):
    rows = pl.ds(pl.multiple_of(core[0] * HALF, HALF), HALF)
    out[...] = dot(turned[rows, :], d_proj[0:NEAR, :]) + dot(turned_next[rows, :], d_proj[NEAR:ALL, :])


def tiles_of():
    for tile in range(HALF // 16 * (E // 128)):
        r, c = divmod(tile, E // 128)
        p, t = divmod(tile, TILES)
        yield r * 16, slice(c * 128, c * 128 + 128), p, slice(t * 16, t * 16 + 16)


def add_body(mine, got, out):
    total = (mine[...] + got[...].astype(f32)).astype(bf16)
    for row, cols, p, rows in tiles_of():
        out[p, rows, :] = total[row : row + 16, cols]
    out[SIDE - 1] = jnp.zeros((TILES * 16, 128), bf16)


def back_body(slope, img_b, next_b, out):
    grad = t_dot(slope[0:NEAR, :], img_b[...]) + t_dot(slope[NEAR:ALL, :], next_b[...])
    out[...] = grad.astype(bf16)


def cube_sum_body(parts, out):
    total = jnp.sum(parts[...].astype(f32), axis=0).astype(bf16)
    for t in range(TILES):
        out[t] = total[t * 16 : t * 16 + 16]
    out[TILES:] = jnp.zeros((SIDE - TILES, 16, 128), bf16)


def grid_sum_body(tiles, out):
    total = jnp.sum(tiles[...].astype(f32), axis=0) * (1.0 / jnp.sqrt(f32(ROWS)))
    out[...] = jnp.broadcast_to(total.astype(bf16)[None], (SIDE, 16, 128))


def cube_spread_body(tiles, out):
    for t in range(TILES):
        out[:, t * 16 : t * 16 + 16, :] = jnp.broadcast_to(tiles[t][None], (SIDE, 16, 128))


def finish_body(d_own, got, late, images, head, d_txt, back, texts, image_out, text_out):
    norm, inv = normalize(dot(images[...], head[...]))
    d_proj = tangent(d_own[...] + got[...] + late[...].astype(f32), norm, inv).astype(bf16)
    image_out[...] = dot_t(d_proj, head[...]).astype(bf16)
    norm, inv = normalize(texts[...].astype(f32))
    text_out[...] = tangent(d_txt[...] + back[...].astype(f32), norm, inv).astype(bf16)


def halves_body(core, mine, got, out):
    first = core[0] * HALF
    second = HALF - first
    for row, cols, p, rows in tiles_of():
        out[pl.ds(pl.multiple_of(first + row, 16), 16), cols] = mine[p, rows, :]
        out[pl.ds(pl.multiple_of(second + row, 16), 16), cols] = got[p, rows, :]


def shards(images, texts, head, log_scale, bias):
    scal = jnp.concatenate([jnp.exp(log_scale), bias])
    core = lax.axis_index("c").astype(jnp.int32).reshape(1)
    other = swapped(images)
    nxt = shifted(images, -1, range(0, COUNT, 2))
    prev = shifted(texts, 2)

    block = (VMEM, (ROWS, E), f32)
    img_n, img_inv, img_b, d_near, d_txt, turned, mark = call(
        near_body, "near",
        ((SMEM, scal), (SMEM, core), (VMEM, images), (VMEM, other), (VMEM, texts), (VMEM, head)),
        ((VMEM, (NEAR, E), f32), (VMEM, (NEAR, 1), f32), (VMEM, (NEAR, E), bf16), (VMEM, (NEAR, E), f32),
         block, (VMEM, (D, NEAR), bf16)),
        (pltpu.VMEM((NEAR, D), bf16),), 1_730_000_000, mark=True)
    next_n, next_inv, next_b, turned_next = call(
        next_body, "next",
        ((VMEM, nxt), (VMEM, head)),
        (block, (VMEM, (ROWS, 1), f32), (VMEM, (ROWS, E), bf16), (VMEM, (D, ROWS), bf16)),
        flops=470_000_000, after=(mark,))
    sent, d_proj, d_own, d_other, d_next, slope = call(
        prev_body, "prev",
        ((SMEM, scal), (SMEM, core), (VMEM, prev), (VMEM, img_n), (VMEM, img_inv), (VMEM, img_b), (VMEM, d_near),
         (VMEM, turned), (VMEM, next_n), (VMEM, next_inv), (VMEM, next_b), (VMEM, turned_next)),
        ((VMEM, (HALF, E), bf16), (VMEM, (ALL, E), bf16), block, block, (VMEM, (ROWS, E), bf16), (VMEM, (ALL, ROWS), bf16)),
        flops=1_530_000_000)
    mine = call(
        half_body, "half",
        ((SMEM, core), (VMEM, d_proj), (VMEM, turned), (VMEM, turned_next)),
        ((VMEM, (HALF, E), f32),), flops=710_000_000)
    part, mark = call(
        add_body, "add", ((VMEM, mine), (VMEM, swapped(sent))), ((VMEM, (SIDE, TILES * 16, 128), bf16),), mark=True)
    d_prev, mark = call(
        back_body, "back", ((VMEM, slope), (VMEM, img_b), (VMEM, next_b)), ((VMEM, (ROWS, E), bf16),),
        flops=400_000_000, after=(mark,), mark=True)
    d_beside = swapped(d_other)
    d_late = shifted(d_next, 1, range(1, COUNT, 2))
    d_back = shifted(d_prev, -2)
    tiles = call(
        cube_sum_body, "cube_sum", ((VMEM, exchange(part, CUBE)),), ((VMEM, (SIDE, 16, 128), bf16),), after=(mark,))
    tiles, mark = call(
        grid_sum_body, "grid_sum", ((VMEM, exchange(tiles, GRID)),), ((VMEM, (SIDE, 16, 128), bf16),),
        flops=40_000_000_000, mark=True)
    grad_image, grad_text, mark = call(
        finish_body, "finish",
        ((VMEM, d_own), (VMEM, d_beside), (VMEM, d_late), (VMEM, images), (VMEM, head), (VMEM, d_txt),
         (VMEM, d_back), (VMEM, texts)),
        ((VMEM, (ROWS, D), bf16), (VMEM, (ROWS, E), bf16)), flops=960_000_000, after=(mark,), mark=True)
    part = call(
        cube_spread_body, "cube_spread", ((VMEM, exchange(tiles, GRID)),),
        ((VMEM, (SIDE, TILES * 16, 128), bf16),), after=(mark,))
    part = exchange(part, CUBE)
    grad_head = call(
        halves_body, "halves", ((SMEM, core), (VMEM, part), (VMEM, swapped(part))), ((VMEM, (D, E), bf16),))
    return (grad_image, grad_text, grad_head)


def solution(mesh):
    grid = Mesh(mesh.devices.reshape(SIZES), AXES)
    in_specs = (P(AXES, None), P(AXES, None), P(), P(), P())
    out_specs = (P(AXES, None), P(AXES, None), P())
    return jax.shard_map(shards, mesh=grid, in_specs=in_specs, out_specs=out_specs, check_vma=False)
```

```python
import jax
import jax.numpy as jnp
from jax import lax
from jax.experimental import pallas as pl
from jax.experimental.pallas import tpu as pltpu
from jax.sharding import Mesh, PartitionSpec as P

ROWS = 320
NEAR = 2 * ROWS
ALL = 3 * ROWS
D = 1152
E = 640
HALF = D // 2
AXES = ("zh", "zl", "x", "yh", "yl", "c")
SIZES = (4, 2, 4, 4, 2, 2)
CUBE = ("zl", "x", "yl")
GRID = ("zh", "yh")
SIDE = 16
TILES = 12
COUNT = 512
f32 = jnp.float32
bf16 = jnp.bfloat16


def shifted(value, steps, sources=None):
    sources = range(COUNT) if sources is None else sources
    return lax.ppermute(value, AXES, [(s, (s + steps) % COUNT) for s in sources])


def swapped(value):
    return lax.ppermute(value, "c", [(0, 1), (1, 0)])


def exchange(value, axes):
    return lax.all_to_all(value, axes, 0, 0)


VMEM = pl.BlockSpec(memory_space=pltpu.VMEM)
SMEM = pl.BlockSpec(memory_space=pltpu.SMEM)


def call(body, name, ins, outs, scratch=(), flops=0, after=(), mark=False):
    size = sum(a.size * a.dtype.itemsize for s, a in ins if s is not SMEM)
    if mark:
        outs = (*outs, (SMEM, (1,), jnp.int32))
    n_in, n_after, n_out = len(ins), len(after), len(outs)

    def run(*refs):
        refs = list(refs)
        if mark:
            refs.pop(n_in + n_after + n_out - 1)[0] = 0
        body(*refs[:n_in], *refs[n_in + n_after :])

    got = pl.pallas_call(
        run,
        out_shape=tuple(jax.ShapeDtypeStruct(dims, dtype) for _, dims, dtype in outs),
        in_specs=[s for s, _ in ins] + [SMEM] * n_after,
        out_specs=tuple(s for s, _, _ in outs),
        scratch_shapes=list(scratch),
        compiler_params=pltpu.CompilerParams(vmem_limit_bytes=16_000_000),
        cost_estimate=pl.CostEstimate(flops=flops, bytes_accessed=size, transcendentals=0),
        name=name,
    )(*(a for _, a in ins), *after)
    return got[0] if len(outs) == 1 else got


def dot(a, b):
    return jnp.dot(a, b, preferred_element_type=f32)


def dot_t(a, b):
    return lax.dot_general(a, b, (((1,), (1,)), ((), ())), preferred_element_type=f32)


def t_dot(a, b):
    return lax.dot_general(a, b, (((0,), (0,)), ((), ())), preferred_element_type=f32)


def normalize(values):
    inv = lax.rsqrt(jnp.sum(values * values, axis=-1, keepdims=True) + 1e-06)
    return values * inv, inv


def tangent(grad, normed, inv):
    return (grad - normed * jnp.sum(normed * grad, axis=-1, keepdims=True)) * inv


def slope_of(img_b, txt_b, scal):
    return scal[0] * jax.nn.sigmoid(scal[0] * dot_t(img_b, txt_b) + scal[1])


def near_body(scal, core, images, other, texts, head, img_n, img_inv, img_b, d_near, own_slope, turned, im):
    im[0:ROWS, :] = images[...]
    im[ROWS:NEAR, :] = other[...]
    txt_b = normalize(texts[...].astype(f32))[0].astype(bf16)
    norm, inv = normalize(dot(im[...], head[...]))
    img_n[...] = norm
    img_inv[...] = inv
    img_b[...] = norm.astype(bf16)
    row = lax.broadcasted_iota(jnp.int32, (NEAR, ROWS), 0)
    col = lax.broadcasted_iota(jnp.int32, (NEAR, ROWS), 1)
    target = jnp.where(row == col, scal[0], 0.0)
    slope = slope_of(img_b[...], txt_b, scal) - target
    own_slope[...] = jnp.where((row < ROWS) | (core[0] == 0), slope, 0.0).astype(bf16)
    d_near[...] = dot(own_slope[...], txt_b)
    turned[...] = im[...].T


def prev_body(scal, core, texts, img_n, img_inv, img_b, d_near, turned,
              part_sent, d_proj, d_own, d_other, prev_b, slope):
    text = normalize(texts[...].astype(f32))[0].astype(bf16)
    prev_b[...] = text
    slope[...] = slope_of(img_b[...], text, scal).astype(bf16)
    grad = dot(slope[...], text) + d_near[...]
    d_own[...] = grad[0:ROWS]
    d_other[...] = grad[ROWS:NEAR].astype(bf16)
    d_proj[...] = tangent(grad, img_n[...], img_inv[...]).astype(bf16)
    second = pl.multiple_of((1 - core[0]) * HALF, HALF)
    part_sent[...] = dot(turned[pl.ds(second, HALF), :], d_proj[...])


def next_body(scal, core, nxt, head, prev_b, part_sent, d_other, sent, d_proj, turned, slope, next_b, d_next):
    norm, inv = normalize(dot(nxt[...], head[...]))
    next_b[...] = norm.astype(bf16)
    on_second = jnp.where(core[0] == 1, 1.0, 0.0)
    slope[...] = (slope_of(next_b[...], prev_b[...], scal) * on_second).astype(bf16)
    grad = dot(slope[...], prev_b[...])
    d_next[...] = grad.astype(bf16)
    d_proj[...] = tangent(grad, norm, inv).astype(bf16)
    turned[...] = nxt[...].T
    second = pl.multiple_of((1 - core[0]) * HALF, HALF)
    sent[0:HALF, :] = (part_sent[...] + dot(turned[pl.ds(second, HALF), :], d_proj[...])).astype(bf16)
    sent[HALF:, :] = d_other[...]


def half_body(core, d_proj, turned, slope, own_slope, img_b, next_proj, next_turned, next_slope, next_b, d_next,
              mine, back, d_txt, d_late):
    rows = pl.ds(pl.multiple_of(core[0] * HALF, HALF), HALF)
    back[...] = (t_dot(slope[...], img_b[...]) + t_dot(next_slope[...], next_b[...])).astype(bf16)
    d_late[...] = d_next[...]
    d_txt[...] = t_dot(own_slope[...], img_b[...])
    mine[...] = dot(turned[rows, :], d_proj[...]) + dot(next_turned[rows, :], next_proj[...])


def tiles_of():
    for tile in range(HALF // 16 * (E // 128)):
        r, c = divmod(tile, E // 128)
        p, t = divmod(tile, TILES)
        yield r * 16, slice(c * 128, c * 128 + 128), p, slice(t * 16, t * 16 + 16)


def add_body(mine, got, d_own, out, d_img):
    total = (mine[...] + got[0:HALF, :].astype(f32)).astype(bf16)
    for row, cols, p, rows in tiles_of():
        out[p, rows, :] = total[row : row + 16, cols]
    out[SIDE - 1] = jnp.zeros((TILES * 16, 128), bf16)
    d_img[...] = d_own[...] + got[HALF:, :].astype(f32)


def cube_sum_body(parts, out):
    total = jnp.sum(parts[...].astype(f32), axis=0).astype(bf16)
    for t in range(TILES):
        out[t] = total[t * 16 : t * 16 + 16]
    out[TILES:] = jnp.zeros((SIDE - TILES, 16, 128), bf16)


def grid_sum_body(tiles, out):
    total = jnp.sum(tiles[...].astype(f32), axis=0) * (1.0 / jnp.sqrt(f32(ROWS)))
    out[...] = jnp.broadcast_to(total.astype(bf16)[None], (SIDE, 16, 128))


def cube_spread_body(tiles, out):
    for t in range(TILES):
        out[:, t * 16 : t * 16 + 16, :] = jnp.broadcast_to(tiles[t][None], (SIDE, 16, 128))


def finish_body(d_img, late, images, head, d_txt, back, texts, image_out, text_out):
    norm, inv = normalize(dot(images[...], head[...]))
    d_proj = tangent(d_img[...] + late[...].astype(f32), norm, inv).astype(bf16)
    image_out[...] = dot_t(d_proj, head[...]).astype(bf16)
    norm, inv = normalize(texts[...].astype(f32))
    text_out[...] = tangent(d_txt[...] + back[...].astype(f32), norm, inv).astype(bf16)


def halves_body(core, mine, got, out):
    first = core[0] * HALF
    second = HALF - first
    for row, cols, p, rows in tiles_of():
        out[pl.ds(pl.multiple_of(first + row, 16), 16), cols] = mine[p, rows, :]
        out[pl.ds(pl.multiple_of(second + row, 16), 16), cols] = got[p, rows, :]


def shards(images, texts, head, log_scale, bias):
    scal = jnp.concatenate([jnp.exp(log_scale), bias])
    core = lax.axis_index("c").astype(jnp.int32).reshape(1)
    other = swapped(images)
    nxt = shifted(images, -1, range(0, COUNT, 2))
    prev = shifted(texts, 2)

    block, words = (VMEM, (ROWS, E), f32), (VMEM, (ROWS, E), bf16)
    rows = (VMEM, (HALF, E), f32)
    img_n, img_inv, img_b, d_near, own_slope, turned = call(
        near_body, "near",
        ((SMEM, scal), (SMEM, core), (VMEM, images), (VMEM, other), (VMEM, texts), (VMEM, head)),
        ((VMEM, (NEAR, E), f32), (VMEM, (NEAR, 1), f32), (VMEM, (NEAR, E), bf16), (VMEM, (NEAR, E), f32),
         (VMEM, (NEAR, ROWS), bf16), (VMEM, (D, NEAR), bf16)),
        (pltpu.VMEM((NEAR, D), bf16),), 1_730_000_000)
    part_sent, d_proj, d_own, d_other, prev_b, slope = call(
        prev_body, "prev",
        ((SMEM, scal), (SMEM, core), (VMEM, prev), (VMEM, img_n), (VMEM, img_inv), (VMEM, img_b), (VMEM, d_near),
         (VMEM, turned)),
        (rows, (VMEM, (NEAR, E), bf16), block, words, words, (VMEM, (NEAR, ROWS), bf16)), flops=40_000_000_000)
    sent, next_proj, next_turned, next_slope, next_b, d_next = call(
        next_body, "next",
        ((SMEM, scal), (SMEM, core), (VMEM, nxt), (VMEM, head), (VMEM, prev_b), (VMEM, part_sent), (VMEM, d_other)),
        ((VMEM, (HALF + ROWS, E), bf16), words, (VMEM, (D, ROWS), bf16), (VMEM, (ROWS, ROWS), bf16), words, words),
        flops=1_000_000_000)
    mine, back, d_txt, d_next = call(
        half_body, "half",
        ((SMEM, core), (VMEM, d_proj), (VMEM, turned), (VMEM, slope), (VMEM, own_slope), (VMEM, img_b), (VMEM, next_proj),
         (VMEM, next_turned), (VMEM, next_slope), (VMEM, next_b), (VMEM, d_next)),
        (rows, words, block, words), flops=1_300_000_000)
    part, d_img = call(
        add_body, "add", ((VMEM, mine), (VMEM, swapped(sent)), (VMEM, d_own)),
        ((VMEM, (SIDE, TILES * 16, 128), bf16), block))
    tiles = call(cube_sum_body, "cube_sum", ((VMEM, exchange(part, CUBE)),), ((VMEM, (SIDE, 16, 128), bf16),))
    d_late = shifted(d_next, 1, range(1, COUNT, 2))
    d_back = shifted(back, -2)
    tiles = call(
        grid_sum_body, "grid_sum", ((VMEM, exchange(tiles, GRID)),), ((VMEM, (SIDE, 16, 128), bf16),),
        flops=40_000_000_000)
    grad_image, grad_text, mark = call(
        finish_body, "finish",
        ((VMEM, d_img), (VMEM, d_late), (VMEM, images), (VMEM, head), (VMEM, d_txt), (VMEM, d_back), (VMEM, texts)),
        ((VMEM, (ROWS, D), bf16), words), flops=960_000_000, mark=True)
    part = call(
        cube_spread_body, "cube_spread", ((VMEM, exchange(tiles, GRID)),),
        ((VMEM, (SIDE, TILES * 16, 128), bf16),), after=(mark,))
    part = exchange(part, CUBE)
    grad_head = call(
        halves_body, "halves", ((SMEM, core), (VMEM, part), (VMEM, swapped(part))), ((VMEM, (D, E), bf16),))
    return (grad_image, grad_text, grad_head)


def solution(mesh):
    grid = Mesh(mesh.devices.reshape(SIZES), AXES)
    in_specs = (P(AXES, None), P(AXES, None), P(), P(), P())
    out_specs = (P(AXES, None), P(AXES, None), P())
    return jax.shard_map(shards, mesh=grid, in_specs=in_specs, out_specs=out_specs, check_vma=False)
```

```python
import jax
import jax.numpy as jnp
from jax import lax
from jax.experimental import pallas as pl
from jax.experimental.pallas import tpu as pltpu
from jax.sharding import Mesh, PartitionSpec as P

ROWS = 320
NEAR = 2 * ROWS
ALL = 3 * ROWS
D = 1152
E = 640
HALF = D // 2
AXES = ("zh", "zl", "x", "yh", "yl", "c")
SIZES = (4, 2, 4, 4, 2, 2)
CUBE = ("zl", "x", "yl")
GRID = ("zh", "yh")
SIDE = 16
TILES = 12
COUNT = 512
f32 = jnp.float32
bf16 = jnp.bfloat16


def shifted(value, steps, sources=None):
    sources = range(COUNT) if sources is None else sources
    return lax.ppermute(value, AXES, [(s, (s + steps) % COUNT) for s in sources])


def swapped(value):
    return lax.ppermute(value, "c", [(0, 1), (1, 0)])


def exchange(value, axes):
    return lax.all_to_all(value, axes, 0, 0)


VMEM = pl.BlockSpec(memory_space=pltpu.VMEM)
SMEM = pl.BlockSpec(memory_space=pltpu.SMEM)


def call(body, name, ins, outs, scratch=(), flops=0, after=(), mark=False):
    size = sum(a.size * a.dtype.itemsize for s, a in ins if s is not SMEM)
    if mark:
        outs = (*outs, (SMEM, (1,), jnp.int32))
    n_in, n_after, n_out = len(ins), len(after), len(outs)

    def run(*refs):
        refs = list(refs)
        if mark:
            refs.pop(n_in + n_after + n_out - 1)[0] = 0
        body(*refs[:n_in], *refs[n_in + n_after :])

    got = pl.pallas_call(
        run,
        out_shape=tuple(jax.ShapeDtypeStruct(dims, dtype) for _, dims, dtype in outs),
        in_specs=[s for s, _ in ins] + [SMEM] * n_after,
        out_specs=tuple(s for s, _, _ in outs),
        scratch_shapes=list(scratch),
        compiler_params=pltpu.CompilerParams(vmem_limit_bytes=16_000_000),
        cost_estimate=pl.CostEstimate(flops=flops, bytes_accessed=size, transcendentals=0),
        name=name,
    )(*(a for _, a in ins), *after)
    return got[0] if len(outs) == 1 else got


def dot(a, b):
    return jnp.dot(a, b, preferred_element_type=f32)


def dot_t(a, b):
    return lax.dot_general(a, b, (((1,), (1,)), ((), ())), preferred_element_type=f32)


def t_dot(a, b):
    return lax.dot_general(a, b, (((0,), (0,)), ((), ())), preferred_element_type=f32)


def normalize(values):
    inv = lax.rsqrt(jnp.sum(values * values, axis=-1, keepdims=True) + 1e-06)
    return values * inv, inv


def tangent(grad, normed, inv):
    return (grad - normed * jnp.sum(normed * grad, axis=-1, keepdims=True)) * inv


def slope_of(img_b, txt_b, scal):
    return scal[0] * jax.nn.sigmoid(scal[0] * dot_t(img_b, txt_b) + scal[1])


def words_body(scal, core, texts, out):
    out[...] = normalize(texts[...].astype(f32))[0].astype(bf16)


def near_body(scal, core, images, other, words, head, img_n, img_inv, img_b, d_near, own_slope, turned, im):
    im[0:ROWS, :] = images[...]
    im[ROWS:NEAR, :] = other[...]
    txt_b = words[...]
    norm, inv = normalize(dot(im[...], head[...]))
    img_n[...] = norm
    img_inv[...] = inv
    img_b[...] = norm.astype(bf16)
    row = lax.broadcasted_iota(jnp.int32, (NEAR, ROWS), 0)
    col = lax.broadcasted_iota(jnp.int32, (NEAR, ROWS), 1)
    target = jnp.where(row == col, scal[0], 0.0)
    slope = slope_of(img_b[...], txt_b, scal) - target
    own_slope[...] = jnp.where((row < ROWS) | (core[0] == 0), slope, 0.0).astype(bf16)
    d_near[...] = dot(own_slope[...], txt_b)
    turned[...] = im[...].T


def prev_body(scal, core, texts, img_n, img_inv, img_b, d_near, turned,
              part_sent, d_proj, d_own, d_other, prev_b, slope):
    text = normalize(texts[...].astype(f32))[0].astype(bf16)
    prev_b[...] = text
    slope[...] = slope_of(img_b[...], text, scal).astype(bf16)
    grad = dot(slope[...], text) + d_near[...]
    d_own[...] = grad[0:ROWS]
    d_other[...] = grad[ROWS:NEAR].astype(bf16)
    d_proj[...] = tangent(grad, img_n[...], img_inv[...]).astype(bf16)
    second = pl.multiple_of((1 - core[0]) * HALF, HALF)
    part_sent[...] = dot(turned[pl.ds(second, HALF), :], d_proj[...])


def next_body(scal, core, nxt, head, prev_b, part_sent, d_other, sent, d_proj, turned, slope, next_b, d_next):
    norm, inv = normalize(dot(nxt[...], head[...]))
    next_b[...] = norm.astype(bf16)
    on_second = jnp.where(core[0] == 1, 1.0, 0.0)
    slope[...] = (slope_of(next_b[...], prev_b[...], scal) * on_second).astype(bf16)
    grad = dot(slope[...], prev_b[...])
    d_next[...] = grad.astype(bf16)
    d_proj[...] = tangent(grad, norm, inv).astype(bf16)
    turned[...] = nxt[...].T
    second = pl.multiple_of((1 - core[0]) * HALF, HALF)
    sent[0:HALF, :] = (part_sent[...] + dot(turned[pl.ds(second, HALF), :], d_proj[...])).astype(bf16)
    sent[HALF:, :] = d_other[...]


def half_body(core, d_proj, turned, slope, own_slope, img_b, next_proj, next_turned, next_slope, next_b, d_next,
              mine, back, d_txt, d_late):
    rows = pl.ds(pl.multiple_of(core[0] * HALF, HALF), HALF)
    back[...] = (t_dot(slope[...], img_b[...]) + t_dot(next_slope[...], next_b[...])).astype(bf16)
    d_late[...] = d_next[...]
    d_txt[...] = t_dot(own_slope[...], img_b[...])
    mine[...] = dot(turned[rows, :], d_proj[...]) + dot(next_turned[rows, :], next_proj[...])


def tiles_of():
    for tile in range(HALF // 16 * (E // 128)):
        r, c = divmod(tile, E // 128)
        p, t = divmod(tile, TILES)
        yield r * 16, slice(c * 128, c * 128 + 128), p, slice(t * 16, t * 16 + 16)


def add_body(mine, got, d_own, out, d_img):
    total = (mine[...] + got[0:HALF, :].astype(f32)).astype(bf16)
    for row, cols, p, rows in tiles_of():
        out[p, rows, :] = total[row : row + 16, cols]
    out[SIDE - 1] = jnp.zeros((TILES * 16, 128), bf16)
    d_img[...] = d_own[...] + got[HALF:, :].astype(f32)


def cube_sum_body(parts, out):
    total = jnp.sum(parts[...].astype(f32), axis=0).astype(bf16)
    for t in range(TILES):
        out[t] = total[t * 16 : t * 16 + 16]
    out[TILES:] = jnp.zeros((SIDE - TILES, 16, 128), bf16)


def grid_sum_body(tiles, out):
    total = jnp.sum(tiles[...].astype(f32), axis=0) * (1.0 / jnp.sqrt(f32(ROWS)))
    out[...] = jnp.broadcast_to(total.astype(bf16)[None], (SIDE, 16, 128))


def cube_spread_body(tiles, out):
    for t in range(TILES):
        out[:, t * 16 : t * 16 + 16, :] = jnp.broadcast_to(tiles[t][None], (SIDE, 16, 128))


def image_body(d_img, late, images, head, out):
    norm, inv = normalize(dot(images[...], head[...]))
    d_proj = tangent(d_img[...] + late[...].astype(f32), norm, inv).astype(bf16)
    out[...] = dot_t(d_proj, head[...]).astype(bf16)


def text_body(d_txt, back, texts, out):
    norm, inv = normalize(texts[...].astype(f32))
    out[...] = tangent(d_txt[...] + back[...].astype(f32), norm, inv).astype(bf16)


def halves_body(core, mine, got, out):
    first = core[0] * HALF
    second = HALF - first
    for row, cols, p, rows in tiles_of():
        out[pl.ds(pl.multiple_of(first + row, 16), 16), cols] = mine[p, rows, :]
        out[pl.ds(pl.multiple_of(second + row, 16), 16), cols] = got[p, rows, :]


def shards(images, texts, head, log_scale, bias):
    scal = jnp.concatenate([jnp.exp(log_scale), bias])
    core = lax.axis_index("c").astype(jnp.int32).reshape(1)
    other = swapped(images)
    nxt = shifted(images, -1, range(0, COUNT, 2))
    prev = shifted(texts, 2)

    block, words = (VMEM, (ROWS, E), f32), (VMEM, (ROWS, E), bf16)
    rows = (VMEM, (HALF, E), f32)
    txt_b = call(
        words_body, "words", ((SMEM, scal), (SMEM, core), (VMEM, texts)), (words,), flops=1_000_000_000)
    img_n, img_inv, img_b, d_near, own_slope, turned = call(
        near_body, "near",
        ((SMEM, scal), (SMEM, core), (VMEM, images), (VMEM, other), (VMEM, txt_b), (VMEM, head)),
        ((VMEM, (NEAR, E), f32), (VMEM, (NEAR, 1), f32), (VMEM, (NEAR, E), bf16), (VMEM, (NEAR, E), f32),
         (VMEM, (NEAR, ROWS), bf16), (VMEM, (D, NEAR), bf16)),
        (pltpu.VMEM((NEAR, D), bf16),), 100_000_000)
    part_sent, d_proj, d_own, d_other, prev_b, slope = call(
        prev_body, "prev",
        ((SMEM, scal), (SMEM, core), (VMEM, prev), (VMEM, img_n), (VMEM, img_inv), (VMEM, img_b), (VMEM, d_near),
         (VMEM, turned)),
        (rows, (VMEM, (NEAR, E), bf16), block, words, words, (VMEM, (NEAR, ROWS), bf16)), flops=40_000_000_000)
    sent, next_proj, next_turned, next_slope, next_b, d_next = call(
        next_body, "next",
        ((SMEM, scal), (SMEM, core), (VMEM, nxt), (VMEM, head), (VMEM, prev_b), (VMEM, part_sent), (VMEM, d_other)),
        ((VMEM, (HALF + ROWS, E), bf16), words, (VMEM, (D, ROWS), bf16), (VMEM, (ROWS, ROWS), bf16), words, words),
        flops=1_000_000_000)
    mine, back, d_txt, d_next = call(
        half_body, "half",
        ((SMEM, core), (VMEM, d_proj), (VMEM, turned), (VMEM, slope), (VMEM, own_slope), (VMEM, img_b), (VMEM, next_proj),
         (VMEM, next_turned), (VMEM, next_slope), (VMEM, next_b), (VMEM, d_next)),
        (rows, words, block, words), flops=1_300_000_000)
    part, d_img = call(
        add_body, "add", ((VMEM, mine), (VMEM, swapped(sent)), (VMEM, d_own)),
        ((VMEM, (SIDE, TILES * 16, 128), bf16), block))
    tiles = call(cube_sum_body, "cube_sum", ((VMEM, exchange(part, CUBE)),), ((VMEM, (SIDE, 16, 128), bf16),))
    d_late = shifted(d_next, 1, range(1, COUNT, 2))
    d_back = shifted(back, -2)
    tiles = call(
        grid_sum_body, "grid_sum", ((VMEM, exchange(tiles, GRID)),), ((VMEM, (SIDE, 16, 128), bf16),),
        flops=40_000_000_000)
    grad_image, image_mark = call(
        image_body, "image", ((VMEM, d_img), (VMEM, d_late), (VMEM, images), (VMEM, head)),
        ((VMEM, (ROWS, D), bf16),), flops=960_000_000, mark=True)
    grad_text, text_mark = call(
        text_body, "text", ((VMEM, d_txt), (VMEM, d_back), (VMEM, texts)), (words,), after=(image_mark,), mark=True)
    part = call(
        cube_spread_body, "cube_spread", ((VMEM, exchange(tiles, GRID)),),
        ((VMEM, (SIDE, TILES * 16, 128), bf16),), after=(text_mark,))
    part = exchange(part, CUBE)
    grad_head = call(
        halves_body, "halves", ((SMEM, core), (VMEM, part), (VMEM, swapped(part))), ((VMEM, (D, E), bf16),))
    return (grad_image, grad_text, grad_head)


def solution(mesh):
    grid = Mesh(mesh.devices.reshape(SIZES), AXES)
    in_specs = (P(AXES, None), P(AXES, None), P(), P(), P())
    out_specs = (P(AXES, None), P(AXES, None), P())
    return jax.shard_map(shards, mesh=grid, in_specs=in_specs, out_specs=out_specs, check_vma=False)
```

```python
import jax
import jax.numpy as jnp
from jax import lax
from jax.experimental import pallas as pl
from jax.experimental.pallas import tpu as pltpu
from jax.sharding import Mesh, PartitionSpec as P

ROWS = 320
NEAR = 2 * ROWS
ALL = 3 * ROWS
D = 1152
E = 640
HALF = D // 2
AXES = ("zh", "zl", "x", "yh", "yl", "c")
SIZES = (4, 2, 4, 4, 2, 2)
CUBE = ("x", "yl", "zl")
GRID = ("zh", "yh")
SIDE = 16
TILES = 12
COUNT = 512
f32 = jnp.float32
bf16 = jnp.bfloat16


def shifted(value, steps, sources=None):
    sources = range(COUNT) if sources is None else sources
    return lax.ppermute(value, AXES, [(s, (s + steps) % COUNT) for s in sources])


def swapped(value):
    return lax.ppermute(value, "c", [(0, 1), (1, 0)])


def exchange(value, axes):
    return lax.all_to_all(value, axes, 0, 0)


VMEM = pl.BlockSpec(memory_space=pltpu.VMEM)
SMEM = pl.BlockSpec(memory_space=pltpu.SMEM)


def call(body, name, ins, outs, scratch=(), flops=0, after=(), mark=False):
    size = sum(a.size * a.dtype.itemsize for s, a in ins if s is not SMEM)
    if mark:
        outs = (*outs, (SMEM, (1,), jnp.int32))
    n_in, n_after, n_out = len(ins), len(after), len(outs)

    def run(*refs):
        refs = list(refs)
        if mark:
            refs.pop(n_in + n_after + n_out - 1)[0] = 0
        body(*refs[:n_in], *refs[n_in + n_after :])

    got = pl.pallas_call(
        run,
        out_shape=tuple(jax.ShapeDtypeStruct(dims, dtype) for _, dims, dtype in outs),
        in_specs=[s for s, _ in ins] + [SMEM] * n_after,
        out_specs=tuple(s for s, _, _ in outs),
        scratch_shapes=list(scratch),
        compiler_params=pltpu.CompilerParams(vmem_limit_bytes=16_000_000),
        cost_estimate=pl.CostEstimate(flops=flops, bytes_accessed=size, transcendentals=0),
        name=name,
    )(*(a for _, a in ins), *after)
    return got[0] if len(outs) == 1 else got


def dot(a, b):
    return jnp.dot(a, b, preferred_element_type=f32)


def dot_t(a, b):
    return lax.dot_general(a, b, (((1,), (1,)), ((), ())), preferred_element_type=f32)


def t_dot(a, b):
    return lax.dot_general(a, b, (((0,), (0,)), ((), ())), preferred_element_type=f32)


def normalize(values):
    inv = lax.rsqrt(jnp.sum(values * values, axis=-1, keepdims=True) + 1e-06)
    return values * inv, inv


def tangent(grad, normed, inv):
    return (grad - normed * jnp.sum(normed * grad, axis=-1, keepdims=True)) * inv


def slope_of(img_b, txt_b, scal):
    return scal[0] * jax.nn.sigmoid(scal[0] * dot_t(img_b, txt_b) + scal[1])


def words_body(scal, core, texts, out):
    out[...] = normalize(texts[...].astype(f32))[0].astype(bf16)


def near_body(scal, core, images, other, words, head, img_n, img_inv, img_b, d_near, own_slope, turned, im):
    im[0:ROWS, :] = images[...]
    im[ROWS:NEAR, :] = other[...]
    txt_b = words[...]
    norm, inv = normalize(dot(im[...], head[...]))
    img_n[...] = norm
    img_inv[...] = inv
    img_b[...] = norm.astype(bf16)
    row = lax.broadcasted_iota(jnp.int32, (NEAR, ROWS), 0)
    col = lax.broadcasted_iota(jnp.int32, (NEAR, ROWS), 1)
    target = jnp.where(row == col, scal[0], 0.0)
    slope = slope_of(img_b[...], txt_b, scal) - target
    own_slope[...] = jnp.where((row < ROWS) | (core[0] == 0), slope, 0.0).astype(bf16)
    d_near[...] = dot(own_slope[...], txt_b)
    turned[...] = im[...].T


def prev_body(scal, core, texts, img_n, img_inv, img_b, d_near, own_slope, turned,
              part_sent, d_proj, d_own, d_other, prev_b, part_back, d_txt):
    text = normalize(texts[...].astype(f32))[0].astype(bf16)
    prev_b[...] = text
    slope = slope_of(img_b[...], text, scal).astype(bf16)
    grad = dot(slope, text) + d_near[...]
    d_own[...] = grad[0:ROWS]
    d_other[...] = grad[ROWS:NEAR].astype(bf16)
    d_proj[...] = tangent(grad, img_n[...], img_inv[...]).astype(bf16)
    second = pl.multiple_of((1 - core[0]) * HALF, HALF)
    part_sent[...] = dot(turned[pl.ds(second, HALF), :], d_proj[...])
    part_back[...] = t_dot(slope, img_b[...])
    d_txt[...] = t_dot(own_slope[...], img_b[...])


def next_body(scal, core, nxt, head, prev_b, part_sent, d_other, sent, d_proj, turned, slope, next_b, d_next):
    norm, inv = normalize(dot(nxt[...], head[...]))
    next_b[...] = norm.astype(bf16)
    on_second = jnp.where(core[0] == 1, 1.0, 0.0)
    slope[...] = (slope_of(next_b[...], prev_b[...], scal) * on_second).astype(bf16)
    grad = dot(slope[...], prev_b[...])
    d_next[...] = grad.astype(bf16)
    d_proj[...] = tangent(grad, norm, inv).astype(bf16)
    turned[...] = nxt[...].T
    second = pl.multiple_of((1 - core[0]) * HALF, HALF)
    sent[0:HALF, :] = (part_sent[...] + dot(turned[pl.ds(second, HALF), :], d_proj[...])).astype(bf16)
    sent[HALF:, :] = d_other[...]


def half_body(core, d_proj, turned, next_proj, next_turned, next_slope, next_b, part_back, d_next, mine, back, d_late):
    rows = pl.ds(pl.multiple_of(core[0] * HALF, HALF), HALF)
    back[...] = (part_back[...] + t_dot(next_slope[...], next_b[...])).astype(bf16)
    d_late[...] = d_next[...]
    mine[...] = dot(turned[rows, :], d_proj[...]) + dot(next_turned[rows, :], next_proj[...])


def tiles_of():
    for tile in range(HALF // 16 * (E // 128)):
        r, c = divmod(tile, E // 128)
        p, t = divmod(tile, TILES)
        yield r * 16, slice(c * 128, c * 128 + 128), p, slice(t * 16, t * 16 + 16)


def add_body(mine, got, d_own, out, d_img):
    total = (mine[...] + got[0:HALF, :].astype(f32)).astype(bf16)
    for row, cols, p, rows in tiles_of():
        out[p, rows, :] = total[row : row + 16, cols]
    out[SIDE - 1] = jnp.zeros((TILES * 16, 128), bf16)
    d_img[...] = d_own[...] + got[HALF:, :].astype(f32)


def cube_sum_body(parts, out):
    total = jnp.sum(parts[...].astype(f32), axis=0).astype(bf16)
    for t in range(TILES):
        out[t] = total[t * 16 : t * 16 + 16]
    out[TILES:] = jnp.zeros((SIDE - TILES, 16, 128), bf16)


def grid_sum_body(tiles, out):
    total = jnp.sum(tiles[...].astype(f32), axis=0) * (1.0 / jnp.sqrt(f32(ROWS)))
    out[...] = jnp.broadcast_to(total.astype(bf16)[None], (SIDE, 16, 128))


def cube_spread_body(tiles, out):
    for t in range(TILES):
        out[:, t * 16 : t * 16 + 16, :] = jnp.broadcast_to(tiles[t][None], (SIDE, 16, 128))


def image_body(d_img, late, images, head, out):
    norm, inv = normalize(dot(images[...], head[...]))
    d_proj = tangent(d_img[...] + late[...].astype(f32), norm, inv).astype(bf16)
    out[...] = dot_t(d_proj, head[...]).astype(bf16)


def text_body(d_txt, back, texts, out):
    norm, inv = normalize(texts[...].astype(f32))
    out[...] = tangent(d_txt[...] + back[...].astype(f32), norm, inv).astype(bf16)


def pass_body(parts, out):
    out[...] = parts[...]


def halves_body(core, mine, got, out):
    first = core[0] * HALF
    second = HALF - first
    for row, cols, p, rows in tiles_of():
        out[pl.ds(pl.multiple_of(first + row, 16), 16), cols] = mine[p, rows, :]
        out[pl.ds(pl.multiple_of(second + row, 16), 16), cols] = got[p, rows, :]


def shards(images, texts, head, log_scale, bias):
    scal = jnp.concatenate([jnp.exp(log_scale), bias])
    core = lax.axis_index("c").astype(jnp.int32).reshape(1)
    other = swapped(images)
    nxt = shifted(images, -1, range(0, COUNT, 2))
    prev = shifted(texts, 2)

    block, words = (VMEM, (ROWS, E), f32), (VMEM, (ROWS, E), bf16)
    rows = (VMEM, (HALF, E), f32)
    txt_b = call(
        words_body, "words", ((SMEM, scal), (SMEM, core), (VMEM, texts)), (words,), flops=1_000_000_000)
    img_n, img_inv, img_b, d_near, own_slope, turned = call(
        near_body, "near",
        ((SMEM, scal), (SMEM, core), (VMEM, images), (VMEM, other), (VMEM, txt_b), (VMEM, head)),
        ((VMEM, (NEAR, E), f32), (VMEM, (NEAR, 1), f32), (VMEM, (NEAR, E), bf16), (VMEM, (NEAR, E), f32),
         (VMEM, (NEAR, ROWS), bf16), (VMEM, (D, NEAR), bf16)),
        (pltpu.VMEM((NEAR, D), bf16),), 100_000_000)
    part_sent, d_proj, d_own, d_other, prev_b, part_back, d_txt = call(
        prev_body, "prev",
        ((SMEM, scal), (SMEM, core), (VMEM, prev), (VMEM, img_n), (VMEM, img_inv), (VMEM, img_b), (VMEM, d_near),
         (VMEM, own_slope), (VMEM, turned)),
        (rows, (VMEM, (NEAR, E), bf16), block, words, words, block, block), flops=40_000_000_000)
    sent, next_proj, next_turned, next_slope, next_b, d_next = call(
        next_body, "next",
        ((SMEM, scal), (SMEM, core), (VMEM, nxt), (VMEM, head), (VMEM, prev_b), (VMEM, part_sent), (VMEM, d_other)),
        ((VMEM, (HALF + ROWS, E), bf16), words, (VMEM, (D, ROWS), bf16), (VMEM, (ROWS, ROWS), bf16), words, words),
        flops=1_000_000_000)
    mine, back, d_next = call(
        half_body, "half",
        ((SMEM, core), (VMEM, d_proj), (VMEM, turned), (VMEM, next_proj), (VMEM, next_turned), (VMEM, next_slope),
         (VMEM, next_b), (VMEM, part_back), (VMEM, d_next)),
        (rows, words, words), flops=900_000_000)
    part, d_img = call(
        add_body, "add", ((VMEM, mine), (VMEM, swapped(sent)), (VMEM, d_own)),
        ((VMEM, (SIDE, TILES * 16, 128), bf16), block))
    tiles = call(cube_sum_body, "cube_sum", ((VMEM, exchange(part, CUBE)),), ((VMEM, (SIDE, 16, 128), bf16),))
    d_late = shifted(d_next, 1, range(1, COUNT, 2))
    d_back = shifted(back, -2)
    tiles = call(
        grid_sum_body, "grid_sum", ((VMEM, exchange(tiles, GRID)),), ((VMEM, (SIDE, 16, 128), bf16),),
        flops=40_000_000_000)
    grad_text, mark = call(
        text_body, "text", ((VMEM, d_txt), (VMEM, d_back), (VMEM, texts)), (words,), mark=True)
    part = call(
        cube_spread_body, "cube_spread", ((VMEM, exchange(tiles, GRID)),),
        ((VMEM, (SIDE, TILES * 16, 128), bf16),), flops=40_000_000_000, after=(mark,))
    grad_image, mark = call(
        image_body, "image", ((VMEM, d_img), (VMEM, d_late), (VMEM, images), (VMEM, head)),
        ((VMEM, (ROWS, D), bf16),), flops=40_000_000_000, mark=True)
    part = call(
        pass_body, "pass", ((VMEM, exchange(part, CUBE)),), ((VMEM, (SIDE, TILES * 16, 128), bf16),), after=(mark,))
    grad_head = call(
        halves_body, "halves", ((SMEM, core), (VMEM, part), (VMEM, swapped(part))), ((VMEM, (D, E), bf16),))
    return (grad_image, grad_text, grad_head)


def solution(mesh):
    grid = Mesh(mesh.devices.reshape(SIZES), AXES)
    in_specs = (P(AXES, None), P(AXES, None), P(), P(), P())
    out_specs = (P(AXES, None), P(AXES, None), P())
    return jax.shard_map(shards, mesh=grid, in_specs=in_specs, out_specs=out_specs, check_vma=False)
```

```python
import jax
import jax.numpy as jnp
from jax import lax
from jax.experimental import pallas as pl
from jax.experimental.pallas import tpu as pltpu
from jax.sharding import Mesh, PartitionSpec as P

ROWS = 320
NEAR = 2 * ROWS
ALL = 3 * ROWS
D = 1152
E = 640
HALF = D // 2
AXES = ("zh", "zl", "x", "yh", "yl", "c")
SIZES = (4, 2, 4, 4, 2, 2)
CUBE = ("x", "yl", "zl")
GRID = ("zh", "yh")
SIDE = 16
TILES = 12
COUNT = 512
f32 = jnp.float32
bf16 = jnp.bfloat16


def shifted(value, steps, sources=None):
    sources = range(COUNT) if sources is None else sources
    return lax.ppermute(value, AXES, [(s, (s + steps) % COUNT) for s in sources])


def swapped(value):
    return lax.ppermute(value, "c", [(0, 1), (1, 0)])


def exchange(value, axes):
    return lax.all_to_all(value, axes, 0, 0)


VMEM = pl.BlockSpec(memory_space=pltpu.VMEM)
SMEM = pl.BlockSpec(memory_space=pltpu.SMEM)


def call(body, name, ins, outs, scratch=(), flops=0, after=(), mark=False):
    size = sum(a.size * a.dtype.itemsize for s, a in ins if s is not SMEM)
    if mark:
        outs = (*outs, (SMEM, (1,), jnp.int32))
    n_in, n_after, n_out = len(ins), len(after), len(outs)

    def run(*refs):
        refs = list(refs)
        if mark:
            refs.pop(n_in + n_after + n_out - 1)[0] = 0
        body(*refs[:n_in], *refs[n_in + n_after :])

    got = pl.pallas_call(
        run,
        out_shape=tuple(jax.ShapeDtypeStruct(dims, dtype) for _, dims, dtype in outs),
        in_specs=[s for s, _ in ins] + [SMEM] * n_after,
        out_specs=tuple(s for s, _, _ in outs),
        scratch_shapes=list(scratch),
        compiler_params=pltpu.CompilerParams(vmem_limit_bytes=16_000_000),
        cost_estimate=pl.CostEstimate(flops=flops, bytes_accessed=size, transcendentals=0),
        name=name,
    )(*(a for _, a in ins), *after)
    return got[0] if len(outs) == 1 else got


def dot(a, b):
    return jnp.dot(a, b, preferred_element_type=f32)


def dot_t(a, b):
    return lax.dot_general(a, b, (((1,), (1,)), ((), ())), preferred_element_type=f32)


def t_dot(a, b):
    return lax.dot_general(a, b, (((0,), (0,)), ((), ())), preferred_element_type=f32)


def normalize(values):
    inv = lax.rsqrt(jnp.sum(values * values, axis=-1, keepdims=True) + 1e-06)
    return values * inv, inv


def tangent(grad, normed, inv):
    return (grad - normed * jnp.sum(normed * grad, axis=-1, keepdims=True)) * inv


def slope_of(img_b, txt_b, scal):
    return scal[0] * jax.nn.sigmoid(scal[0] * dot_t(img_b, txt_b) + scal[1])


def words_body(scal, core, texts, out):
    out[...] = normalize(texts[...].astype(f32))[0].astype(bf16)


def near_body(scal, core, images, other, words, head, img_n, img_inv, img_b, d_near, own_slope, turned, im):
    im[0:ROWS, :] = images[...]
    im[ROWS:NEAR, :] = other[...]
    txt_b = words[...]
    norm, inv = normalize(dot(im[...], head[...]))
    img_n[...] = norm
    img_inv[...] = inv
    img_b[...] = norm.astype(bf16)
    row = lax.broadcasted_iota(jnp.int32, (NEAR, ROWS), 0)
    col = lax.broadcasted_iota(jnp.int32, (NEAR, ROWS), 1)
    target = jnp.where(row == col, scal[0], 0.0)
    slope = slope_of(img_b[...], txt_b, scal) - target
    own_slope[...] = jnp.where((row < ROWS) | (core[0] == 0), slope, 0.0).astype(bf16)
    d_near[...] = dot(own_slope[...], txt_b)
    turned[...] = im[...].T


def prev_body(scal, core, texts, img_n, img_inv, img_b, d_near, own_slope, turned,
              part_sent, d_proj, d_own, d_other, prev_b, part_back, d_txt):
    text = normalize(texts[...].astype(f32))[0].astype(bf16)
    prev_b[...] = text
    slope = slope_of(img_b[...], text, scal).astype(bf16)
    grad = dot(slope, text) + d_near[...]
    d_own[...] = grad[0:ROWS]
    d_other[...] = grad[ROWS:NEAR].astype(bf16)
    d_proj[...] = tangent(grad, img_n[...], img_inv[...]).astype(bf16)
    second = pl.multiple_of((1 - core[0]) * HALF, HALF)
    part_sent[...] = dot(turned[pl.ds(second, HALF), :], d_proj[...])
    part_back[...] = t_dot(slope, img_b[...])
    d_txt[...] = t_dot(own_slope[...], img_b[...])


def next_body(scal, core, nxt, head, prev_b, part_sent, d_other, sent, d_proj, turned, slope, next_b, d_next):
    norm, inv = normalize(dot(nxt[...], head[...]))
    next_b[...] = norm.astype(bf16)
    on_second = jnp.where(core[0] == 1, 1.0, 0.0)
    slope[...] = (slope_of(next_b[...], prev_b[...], scal) * on_second).astype(bf16)
    grad = dot(slope[...], prev_b[...])
    d_next[...] = grad.astype(bf16)
    d_proj[...] = tangent(grad, norm, inv).astype(bf16)
    turned[...] = nxt[...].T
    second = pl.multiple_of((1 - core[0]) * HALF, HALF)
    sent[0:HALF, :] = (part_sent[...] + dot(turned[pl.ds(second, HALF), :], d_proj[...])).astype(bf16)
    sent[HALF:, :] = d_other[...]


def half_body(core, d_proj, turned, next_proj, next_turned, next_slope, next_b, part_back, d_next, mine, back, d_late):
    rows = pl.ds(pl.multiple_of(core[0] * HALF, HALF), HALF)
    back[...] = (part_back[...] + t_dot(next_slope[...], next_b[...])).astype(bf16)
    d_late[...] = d_next[...]
    mine[...] = dot(turned[rows, :], d_proj[...]) + dot(next_turned[rows, :], next_proj[...])


def tiles_of():
    for tile in range(HALF // 16 * (E // 128)):
        r, c = divmod(tile, E // 128)
        p, t = divmod(tile, TILES)
        yield r * 16, slice(c * 128, c * 128 + 128), p, slice(t * 16, t * 16 + 16)


def add_body(mine, got, d_own, out, d_img):
    total = (mine[...] + got[0:HALF, :].astype(f32)).astype(bf16)
    for row, cols, p, rows in tiles_of():
        out[p, rows, :] = total[row : row + 16, cols]
    out[SIDE - 1] = jnp.zeros((TILES * 16, 128), bf16)
    d_img[...] = d_own[...] + got[HALF:, :].astype(f32)


def cube_sum_body(parts, out):
    total = jnp.sum(parts[...].astype(f32), axis=0).astype(bf16)
    for t in range(TILES):
        out[t] = total[t * 16 : t * 16 + 16]
    out[TILES:] = jnp.zeros((SIDE - TILES, 16, 128), bf16)


def grid_sum_body(tiles, out):
    total = jnp.sum(tiles[...].astype(f32), axis=0) * (1.0 / jnp.sqrt(f32(ROWS)))
    out[...] = jnp.broadcast_to(total.astype(bf16)[None], (SIDE, 16, 128))


def cube_spread_body(tiles, out):
    for t in range(TILES):
        out[:, t * 16 : t * 16 + 16, :] = jnp.broadcast_to(tiles[t][None], (SIDE, 16, 128))


def image_body(d_img, late, images, head, out):
    norm, inv = normalize(dot(images[...], head[...]))
    d_proj = tangent(d_img[...] + late[...].astype(f32), norm, inv).astype(bf16)
    out[...] = dot_t(d_proj, head[...]).astype(bf16)


def text_body(d_txt, back, texts, out):
    norm, inv = normalize(texts[...].astype(f32))
    out[...] = tangent(d_txt[...] + back[...].astype(f32), norm, inv).astype(bf16)


def pass_body(parts, out):
    out[...] = parts[...]


def put_half(parts, out, start, half, sem):
    for row, cols, p, rows in tiles_of():
        half[row : row + 16, cols] = parts[p, rows, :]
    rows = pl.ds(pl.multiple_of(start, HALF), HALF)
    copy = pltpu.make_async_copy(half, out.at[rows, :], sem)
    copy.start()
    copy.wait()


def first_body(core, parts, out, half, sem):
    put_half(parts, out, core[0] * HALF, half, sem)


def second_body(core, parts, held, out, half, sem):
    put_half(parts, out, (1 - core[0]) * HALF, half, sem)


def halves(core, mine, got):
    anywhere = pl.BlockSpec(memory_space=pl.ANY)
    common = dict(
        out_shape=jax.ShapeDtypeStruct((D, E), bf16),
        out_specs=anywhere,
        scratch_shapes=[pltpu.VMEM((HALF, E), bf16), pltpu.SemaphoreType.DMA],
        compiler_params=pltpu.CompilerParams(vmem_limit_bytes=16_000_000),
        cost_estimate=pl.CostEstimate(flops=0, bytes_accessed=HALF * E * 4, transcendentals=0),
    )
    held = pl.pallas_call(first_body, in_specs=[SMEM, VMEM], name="first_half", **common)(core, mine)
    return pl.pallas_call(
        second_body, in_specs=[SMEM, VMEM, anywhere], input_output_aliases={2: 0}, name="second_half", **common
    )(core, got, held)


def shards(images, texts, head, log_scale, bias):
    scal = jnp.concatenate([jnp.exp(log_scale), bias])
    core = lax.axis_index("c").astype(jnp.int32).reshape(1)
    other = swapped(images)
    nxt = shifted(images, -1, range(0, COUNT, 2))
    prev = shifted(texts, 2)

    block, words = (VMEM, (ROWS, E), f32), (VMEM, (ROWS, E), bf16)
    rows = (VMEM, (HALF, E), f32)
    txt_b = call(
        words_body, "words", ((SMEM, scal), (SMEM, core), (VMEM, texts)), (words,), flops=1_000_000_000)
    img_n, img_inv, img_b, d_near, own_slope, turned = call(
        near_body, "near",
        ((SMEM, scal), (SMEM, core), (VMEM, images), (VMEM, other), (VMEM, txt_b), (VMEM, head)),
        ((VMEM, (NEAR, E), f32), (VMEM, (NEAR, 1), f32), (VMEM, (NEAR, E), bf16), (VMEM, (NEAR, E), f32),
         (VMEM, (NEAR, ROWS), bf16), (VMEM, (D, NEAR), bf16)),
        (pltpu.VMEM((NEAR, D), bf16),), 100_000_000)
    part_sent, d_proj, d_own, d_other, prev_b, part_back, d_txt = call(
        prev_body, "prev",
        ((SMEM, scal), (SMEM, core), (VMEM, prev), (VMEM, img_n), (VMEM, img_inv), (VMEM, img_b), (VMEM, d_near),
         (VMEM, own_slope), (VMEM, turned)),
        (rows, (VMEM, (NEAR, E), bf16), block, words, words, block, block), flops=40_000_000_000)
    sent, next_proj, next_turned, next_slope, next_b, d_next = call(
        next_body, "next",
        ((SMEM, scal), (SMEM, core), (VMEM, nxt), (VMEM, head), (VMEM, prev_b), (VMEM, part_sent), (VMEM, d_other)),
        ((VMEM, (HALF + ROWS, E), bf16), words, (VMEM, (D, ROWS), bf16), (VMEM, (ROWS, ROWS), bf16), words, words),
        flops=1_000_000_000)
    mine, back, d_next = call(
        half_body, "half",
        ((SMEM, core), (VMEM, d_proj), (VMEM, turned), (VMEM, next_proj), (VMEM, next_turned), (VMEM, next_slope),
         (VMEM, next_b), (VMEM, part_back), (VMEM, d_next)),
        (rows, words, words), flops=900_000_000)
    part, d_img = call(
        add_body, "add", ((VMEM, mine), (VMEM, swapped(sent)), (VMEM, d_own)),
        ((VMEM, (SIDE, TILES * 16, 128), bf16), block))
    tiles = call(cube_sum_body, "cube_sum", ((VMEM, exchange(part, CUBE)),), ((VMEM, (SIDE, 16, 128), bf16),))
    d_late = shifted(d_next, 1, range(1, COUNT, 2))
    d_back = shifted(back, -2)
    tiles = call(
        grid_sum_body, "grid_sum", ((VMEM, exchange(tiles, GRID)),), ((VMEM, (SIDE, 16, 128), bf16),),
        flops=40_000_000_000)
    grad_text, mark = call(
        text_body, "text", ((VMEM, d_txt), (VMEM, d_back), (VMEM, texts)), (words,), mark=True)
    part = call(
        cube_spread_body, "cube_spread", ((VMEM, exchange(tiles, GRID)),),
        ((VMEM, (SIDE, TILES * 16, 128), bf16),), flops=40_000_000_000, after=(mark,))
    grad_image, mark = call(
        image_body, "image", ((VMEM, d_img), (VMEM, d_late), (VMEM, images), (VMEM, head)),
        ((VMEM, (ROWS, D), bf16),), flops=40_000_000_000, mark=True)
    part = call(
        pass_body, "pass", ((VMEM, exchange(part, CUBE)),), ((VMEM, (SIDE, TILES * 16, 128), bf16),), after=(mark,))
    grad_head = halves(core, part, swapped(part))
    return (grad_image, grad_text, grad_head)


def solution(mesh):
    grid = Mesh(mesh.devices.reshape(SIZES), AXES)
    in_specs = (P(AXES, None), P(AXES, None), P(), P(), P())
    out_specs = (P(AXES, None), P(AXES, None), P())
    return jax.shard_map(shards, mesh=grid, in_specs=in_specs, out_specs=out_specs, check_vma=False)
```

```python
import jax
import jax.numpy as jnp
from jax import lax
from jax.experimental import pallas as pl
from jax.experimental.pallas import tpu as pltpu
from jax.sharding import Mesh, PartitionSpec as P

ROWS = 320
NEAR = 2 * ROWS
ALL = 3 * ROWS
D = 1152
E = 640
HALF = D // 2
AXES = ("zh", "zl", "x", "yh", "yl", "c")
SIZES = (4, 2, 4, 4, 2, 2)
CUBE = ("x", "yl", "zl")
GRID = ("zh", "yh")
SIDE = 16
TILES = 12
COUNT = 512
f32 = jnp.float32
bf16 = jnp.bfloat16


def shifted(value, steps, sources=None):
    sources = range(COUNT) if sources is None else sources
    return lax.ppermute(value, AXES, [(s, (s + steps) % COUNT) for s in sources])


def swapped(value):
    return lax.ppermute(value, "c", [(0, 1), (1, 0)])


def exchange(value, axes):
    return lax.all_to_all(value, axes, 0, 0)


VMEM = pl.BlockSpec(memory_space=pltpu.VMEM)
SMEM = pl.BlockSpec(memory_space=pltpu.SMEM)


def call(body, name, ins, outs, scratch=(), flops=0, after=(), mark=False):
    size = sum(a.size * a.dtype.itemsize for s, a in ins if s is not SMEM)
    if mark:
        outs = (*outs, (SMEM, (1,), jnp.int32))
    n_in, n_after, n_out = len(ins), len(after), len(outs)

    def run(*refs):
        refs = list(refs)
        if mark:
            refs.pop(n_in + n_after + n_out - 1)[0] = 0
        body(*refs[:n_in], *refs[n_in + n_after :])

    got = pl.pallas_call(
        run,
        out_shape=tuple(jax.ShapeDtypeStruct(dims, dtype) for _, dims, dtype in outs),
        in_specs=[s for s, _ in ins] + [SMEM] * n_after,
        out_specs=tuple(s for s, _, _ in outs),
        scratch_shapes=list(scratch),
        compiler_params=pltpu.CompilerParams(vmem_limit_bytes=16_000_000),
        cost_estimate=pl.CostEstimate(flops=flops, bytes_accessed=size, transcendentals=0),
        name=name,
    )(*(a for _, a in ins), *after)
    return got[0] if len(outs) == 1 else got


def dot(a, b):
    return jnp.dot(a, b, preferred_element_type=f32)


def dot_t(a, b):
    return lax.dot_general(a, b, (((1,), (1,)), ((), ())), preferred_element_type=f32)


def t_dot(a, b):
    return lax.dot_general(a, b, (((0,), (0,)), ((), ())), preferred_element_type=f32)


def normalize(values):
    inv = lax.rsqrt(jnp.sum(values * values, axis=-1, keepdims=True) + 1e-06)
    return values * inv, inv


def tangent(grad, normed, inv):
    return (grad - normed * jnp.sum(normed * grad, axis=-1, keepdims=True)) * inv


def slope_of(img_b, txt_b, scal):
    return scal[0] * jax.nn.sigmoid(scal[0] * dot_t(img_b, txt_b) + scal[1])


def words_body(scal, core, texts, out):
    out[...] = normalize(texts[...].astype(f32))[0].astype(bf16)


def near_body(scal, core, images, other, words, head, img_n, img_inv, img_b, d_near, own_slope, turned, im):
    im[0:ROWS, :] = images[...]
    im[ROWS:NEAR, :] = other[...]
    txt_b = words[...]
    norm, inv = normalize(dot(im[...], head[...]))
    img_n[...] = norm
    img_inv[...] = inv
    img_b[...] = norm.astype(bf16)
    row = lax.broadcasted_iota(jnp.int32, (NEAR, ROWS), 0)
    col = lax.broadcasted_iota(jnp.int32, (NEAR, ROWS), 1)
    target = jnp.where(row == col, scal[0], 0.0)
    slope = slope_of(img_b[...], txt_b, scal) - target
    own_slope[...] = jnp.where((row < ROWS) | (core[0] == 0), slope, 0.0).astype(bf16)
    d_near[...] = dot(own_slope[...], txt_b)
    turned[...] = im[...].T


def prev_body(scal, core, texts, img_n, img_inv, img_b, d_near, own_slope, turned,
              part_sent, d_proj, d_own, d_other, prev_b, part_back, d_txt):
    text = normalize(texts[...].astype(f32))[0].astype(bf16)
    prev_b[...] = text
    slope = slope_of(img_b[...], text, scal).astype(bf16)
    grad = dot(slope, text) + d_near[...]
    d_own[...] = grad[0:ROWS]
    d_other[...] = grad[ROWS:NEAR].astype(bf16)
    d_proj[...] = tangent(grad, img_n[...], img_inv[...]).astype(bf16)
    second = pl.multiple_of((1 - core[0]) * HALF, HALF)
    part_sent[...] = dot(turned[pl.ds(second, HALF), :], d_proj[...])
    part_back[...] = t_dot(slope, img_b[...])
    d_txt[...] = t_dot(own_slope[...], img_b[...])


def next_body(scal, core, nxt, head, prev_b, part_sent, d_other, sent, d_proj, turned, slope, next_b, d_next):
    norm, inv = normalize(dot(nxt[...], head[...]))
    next_b[...] = norm.astype(bf16)
    on_second = jnp.where(core[0] == 1, 1.0, 0.0)
    slope[...] = (slope_of(next_b[...], prev_b[...], scal) * on_second).astype(bf16)
    grad = dot(slope[...], prev_b[...])
    d_next[...] = grad.astype(bf16)
    d_proj[...] = tangent(grad, norm, inv).astype(bf16)
    turned[...] = nxt[...].T
    second = pl.multiple_of((1 - core[0]) * HALF, HALF)
    sent[0:HALF, :] = (part_sent[...] + dot(turned[pl.ds(second, HALF), :], d_proj[...])).astype(bf16)
    sent[HALF:, :] = d_other[...]


def half_body(core, d_proj, turned, next_proj, next_turned, next_slope, next_b, part_back, d_next, mine, back, d_late):
    rows = pl.ds(pl.multiple_of(core[0] * HALF, HALF), HALF)
    back[...] = (part_back[...] + t_dot(next_slope[...], next_b[...])).astype(bf16)
    d_late[...] = d_next[...]
    mine[...] = dot(turned[rows, :], d_proj[...]) + dot(next_turned[rows, :], next_proj[...])


def tiles_of():
    for tile in range(HALF // 16 * (E // 128)):
        r, c = divmod(tile, E // 128)
        p, t = divmod(tile, TILES)
        yield r * 16, slice(c * 128, c * 128 + 128), p, slice(t * 16, t * 16 + 16)


def add_body(mine, got, d_own, out, d_img):
    total = (mine[...] + got[0:HALF, :].astype(f32)).astype(bf16)
    for row, cols, p, rows in tiles_of():
        out[p, rows, :] = total[row : row + 16, cols]
    out[SIDE - 1] = jnp.zeros((TILES * 16, 128), bf16)
    d_img[...] = d_own[...] + got[HALF:, :].astype(f32)


def cube_sum_body(parts, out):
    total = jnp.sum(parts[...].astype(f32), axis=0).astype(bf16)
    for t in range(TILES):
        out[t] = total[t * 16 : t * 16 + 16]
    out[TILES:] = jnp.zeros((SIDE - TILES, 16, 128), bf16)


def grid_sum_body(tiles, out):
    total = jnp.sum(tiles[...].astype(f32), axis=0) * (1.0 / jnp.sqrt(f32(ROWS)))
    out[...] = jnp.broadcast_to(total.astype(bf16)[None], (SIDE, 16, 128))


def cube_spread_body(tiles, out):
    for t in range(TILES):
        out[:, t * 16 : t * 16 + 16, :] = jnp.broadcast_to(tiles[t][None], (SIDE, 16, 128))


def image_body(d_img, late, images, head, out):
    norm, inv = normalize(dot(images[...], head[...]))
    d_proj = tangent(d_img[...] + late[...].astype(f32), norm, inv).astype(bf16)
    out[...] = dot_t(d_proj, head[...]).astype(bf16)


def text_body(d_txt, back, texts, out):
    norm, inv = normalize(texts[...].astype(f32))
    out[...] = tangent(d_txt[...] + back[...].astype(f32), norm, inv).astype(bf16)


def pass_body(parts, out):
    out[...] = parts[0 : SIDE - 1]


def put_half(parts, out, start, half, sem):
    for row, cols, p, rows in tiles_of():
        half[row : row + 16, cols] = parts[p, rows, :]
    rows = pl.ds(pl.multiple_of(start, HALF), HALF)
    copy = pltpu.make_async_copy(half, out.at[rows, :], sem)
    copy.start()
    copy.wait()


def first_body(core, parts, out, half, sem):
    put_half(parts, out, core[0] * HALF, half, sem)


def second_body(core, parts, held, out, half, sem):
    put_half(parts, out, (1 - core[0]) * HALF, half, sem)


def halves(core, mine, got):
    anywhere = pl.BlockSpec(memory_space=pl.ANY)
    common = dict(
        out_shape=jax.ShapeDtypeStruct((D, E), bf16),
        out_specs=anywhere,
        scratch_shapes=[pltpu.VMEM((HALF, E), bf16), pltpu.SemaphoreType.DMA],
        compiler_params=pltpu.CompilerParams(vmem_limit_bytes=16_000_000),
        cost_estimate=pl.CostEstimate(flops=0, bytes_accessed=HALF * E * 4, transcendentals=0),
    )
    held = pl.pallas_call(first_body, in_specs=[SMEM, VMEM], name="first_half", **common)(core, mine)
    return pl.pallas_call(
        second_body, in_specs=[SMEM, VMEM, anywhere], input_output_aliases={2: 0}, name="second_half", **common
    )(core, got, held)


def shards(images, texts, head, log_scale, bias):
    scal = jnp.concatenate([jnp.exp(log_scale), bias])
    core = lax.axis_index("c").astype(jnp.int32).reshape(1)
    other = swapped(images)
    nxt = shifted(images, -1, range(0, COUNT, 2))
    prev = shifted(texts, 2)

    block, words = (VMEM, (ROWS, E), f32), (VMEM, (ROWS, E), bf16)
    rows = (VMEM, (HALF, E), f32)
    txt_b = call(
        words_body, "words", ((SMEM, scal), (SMEM, core), (VMEM, texts)), (words,), flops=1_000_000_000)
    img_n, img_inv, img_b, d_near, own_slope, turned = call(
        near_body, "near",
        ((SMEM, scal), (SMEM, core), (VMEM, images), (VMEM, other), (VMEM, txt_b), (VMEM, head)),
        ((VMEM, (NEAR, E), f32), (VMEM, (NEAR, 1), f32), (VMEM, (NEAR, E), bf16), (VMEM, (NEAR, E), f32),
         (VMEM, (NEAR, ROWS), bf16), (VMEM, (D, NEAR), bf16)),
        (pltpu.VMEM((NEAR, D), bf16),), 100_000_000)
    part_sent, d_proj, d_own, d_other, prev_b, part_back, d_txt = call(
        prev_body, "prev",
        ((SMEM, scal), (SMEM, core), (VMEM, prev), (VMEM, img_n), (VMEM, img_inv), (VMEM, img_b), (VMEM, d_near),
         (VMEM, own_slope), (VMEM, turned)),
        (rows, (VMEM, (NEAR, E), bf16), block, words, words, block, block), flops=40_000_000_000)
    sent, next_proj, next_turned, next_slope, next_b, d_next = call(
        next_body, "next",
        ((SMEM, scal), (SMEM, core), (VMEM, nxt), (VMEM, head), (VMEM, prev_b), (VMEM, part_sent), (VMEM, d_other)),
        ((VMEM, (HALF + ROWS, E), bf16), words, (VMEM, (D, ROWS), bf16), (VMEM, (ROWS, ROWS), bf16), words, words),
        flops=1_000_000_000)
    mine, back, d_next = call(
        half_body, "half",
        ((SMEM, core), (VMEM, d_proj), (VMEM, turned), (VMEM, next_proj), (VMEM, next_turned), (VMEM, next_slope),
         (VMEM, next_b), (VMEM, part_back), (VMEM, d_next)),
        (rows, words, words), flops=900_000_000)
    part, d_img = call(
        add_body, "add", ((VMEM, mine), (VMEM, swapped(sent)), (VMEM, d_own)),
        ((VMEM, (SIDE, TILES * 16, 128), bf16), block))
    tiles = call(cube_sum_body, "cube_sum", ((VMEM, exchange(part, CUBE)),), ((VMEM, (SIDE, 16, 128), bf16),))
    d_late = shifted(d_next, 1, range(1, COUNT, 2))
    d_back = shifted(back, -2)
    tiles = call(
        grid_sum_body, "grid_sum", ((VMEM, exchange(tiles, GRID)),), ((VMEM, (SIDE, 16, 128), bf16),),
        flops=40_000_000_000)
    grad_text, mark = call(
        text_body, "text", ((VMEM, d_txt), (VMEM, d_back), (VMEM, texts)), (words,), mark=True)
    part = call(
        cube_spread_body, "cube_spread", ((VMEM, exchange(tiles, GRID)),),
        ((VMEM, (SIDE, TILES * 16, 128), bf16),), flops=40_000_000_000, after=(mark,))
    grad_image, mark = call(
        image_body, "image", ((VMEM, d_img), (VMEM, d_late), (VMEM, images), (VMEM, head)),
        ((VMEM, (ROWS, D), bf16),), flops=40_000_000_000, mark=True)
    part = call(
        pass_body, "pass", ((VMEM, exchange(part, CUBE)),), ((VMEM, (SIDE - 1, TILES * 16, 128), bf16),), after=(mark,))
    grad_head = halves(core, part, swapped(part))
    return (grad_image, grad_text, grad_head)


def solution(mesh):
    grid = Mesh(mesh.devices.reshape(SIZES), AXES)
    in_specs = (P(AXES, None), P(AXES, None), P(), P(), P())
    out_specs = (P(AXES, None), P(AXES, None), P())
    return jax.shard_map(shards, mesh=grid, in_specs=in_specs, out_specs=out_specs, check_vma=False)
```
